32 devices in a mesh: fsdp: 4 (over y, core), ctx: 8 (over z, x).
Axes of the slice: x: 2, y: 2, z: 4, core: 2. Of those that a mesh axis runs over, the one named last changes fastest.
Arguments:
- block_input: bfloat16 [4, 1024, 1024], P('fsdp', 'ctx'), may hold values from -12 to 12
- positions: int32 [4, 1024], P('fsdp', 'ctx'), may hold values from 0 to 999, as said below
- attn_norm_gain: bfloat16 [1024], replicated, may hold values from 0.099609375 to 1.8984375
- w_query: bfloat16 [1024, 2048], P('fsdp'), may hold values from -0.1875 to 0.1875
- key_projection: bfloat16 [1024, 1024], P('fsdp'), may hold values from -0.1875 to 0.1875
- value_projection: bfloat16 [1024, 1024], P('fsdp'), may hold values from -0.1875 to 0.1875
- query_norm_gain: bfloat16 [128], replicated, may hold values from 0.5 to 2
- key_norm_gain: bfloat16 [128], replicated, may hold values from 0.5 to 2
- output_projection: bfloat16 [2048, 1024], P('fsdp'), may hold values from -0.75 to 0.75
- ffn_norm_gain: bfloat16 [1024], replicated, may hold values from 0.099609375 to 1.8984375
- w_gate: bfloat16 [1024, 3072], P('fsdp'), may hold values from -0.1875 to 0.1875
- w_up: bfloat16 [1024, 3072], P('fsdp'), may hold values from -0.1875 to 0.1875
- w_down: bfloat16 [3072, 1024], P('fsdp'), may hold values from -0.109375 to 0.109375
- out_cotangent: bfloat16 [4, 1024, 1024], P('fsdp', 'ctx'), may hold values from -6 to 6
Outputs:
- block_output: bfloat16 [4, 1024, 1024], P('fsdp', 'ctx')
- input_grad: float32 [4, 1024, 1024], P('fsdp', 'ctx')
- attn_gain_grad: float32 [1024], replicated
- query_weight_grad: float32 [1024, 2048], P('fsdp')
- key_weight_grad: float32 [1024, 1024], P('fsdp')
- value_weight_grad: float32 [1024, 1024], P('fsdp')
- query_gain_grad: float32 [128], replicated
- key_gain_grad: float32 [128], replicated
- output_weight_grad: float32 [2048, 1024], P('fsdp')
- ffn_gain_grad: float32 [1024], replicated
- gate_weight_grad: float32 [1024, 3072], P('fsdp')
- up_weight_grad: float32 [1024, 3072], P('fsdp')
- down_weight_grad: float32 [3072, 1024], P('fsdp')
The draws below stay inside these ranges and needn't reach their ends.
Inputs may be any that keep to these rules, and one draw needn't show every extreme that they name: Each sequence is a run of documents: positions count 0, 1, 2, ... within a document and restart at 0 where a new one begins. Every document has at most 1000 tokens and the longest has exactly 1000; all but a sequence's last have at least 102.
All inputs are finite; a program needn't handle non-finite values.
Results may differ from the reference program's by a relative error of at most 0.02.
Values may be sent and summed in bfloat16 or wider, within the bound.
A program may use at most 320 MiB of HBM per device.

```python
import math
import jax
import jax.numpy as jnp
from jax import lax

MODEL_WIDTH = 1024
QUERY_HEADS = 16
KEY_VALUE_HEADS = 8
HEAD_SIZE = 128
FF = 3072
SEQUENCE_LENGTH = 1024
SEQS = 4
DOC_LO = 102
DOC_HI = 1000
N_CTX = 8


def draw_block_input(key, part):
    subkeys = jax.random.split(jax.random.fold_in(key, 7), 3)
    row_scale = jnp.exp(jax.random.uniform(subkeys[0], (SEQS, SEQUENCE_LENGTH, 1), jnp.float32, math.log(0.3), math.log(3.0)))
    column_scale = jnp.exp(jax.random.uniform(subkeys[1], (1, 1, MODEL_WIDTH), jnp.float32, math.log(0.3), math.log(3.0)))
    values = jax.random.normal(subkeys[2], (SEQS, SEQUENCE_LENGTH, MODEL_WIDTH), jnp.float32) * row_scale * column_scale
    return jnp.clip(values, -12.0, 12.0).astype(jnp.bfloat16)


def head_gain(key, salt):
    subkey = jax.random.fold_in(key, salt)
    gains = jnp.exp(jax.random.uniform(subkey, (HEAD_SIZE,), jnp.float32, math.log(0.5), math.log(2.0)))
    return gains.astype(jnp.bfloat16)


def draw_query_norm_gain(key, part):
    return head_gain(key, 11)


def draw_key_norm_gain(key, part):
    return head_gain(key, 13)


def draw_positions(key, part):
    doc_count = SEQUENCE_LENGTH // DOC_LO + 1
    subkeys = jax.random.split(jax.random.fold_in(key, 3), SEQS)
    lengths = jax.vmap(lambda seq_key: jax.random.randint(seq_key, (doc_count,), DOC_LO, DOC_HI + 1))(subkeys)
    lengths = lengths.astype(jnp.int32).at[0, 0].set(DOC_HI)
    doc_ends = jnp.cumsum(lengths, axis=1)
    starts = doc_ends - lengths
    token_ids = jnp.arange(SEQUENCE_LENGTH, dtype=jnp.int32)
    inside = starts[:, None, :] <= token_ids[None, :, None]
    last_start = jnp.max(jnp.where(inside, starts[:, None, :], 0), axis=2)
    return (token_ids[None, :] - last_start).astype(jnp.int32)


def block_levels(own_key, shape, pieces, least, high):
    loudness, own = 1.0, jax.random.fold_in(own_key, 6)
    for axis_at, parts in pieces:
        heights = jnp.exp(jax.random.uniform(jax.random.fold_in(own, axis_at), (parts,), jnp.float32, least / len(pieces), high / len(pieces)))
        loudness = loudness * jnp.repeat(heights, shape[axis_at] // parts).reshape([-1 if axis == axis_at else 1 for axis in range(len(shape))])
    return loudness


def centred(rng, extent, deviation, most, cuts=(), kind=jnp.bfloat16):
    loudness = block_levels(rng, extent, cuts, -0.22, 0.18) if cuts else 1.0
    values = jax.random.normal(rng, extent, jnp.float32) * deviation * loudness
    return jnp.minimum(jnp.maximum(values, -most), most).astype(kind)


def setup_inputs(seed: int = 0) -> dict:
    seeds = jax.random.split(jax.random.key(seed), 15)
    block_input = draw_block_input(jax.random.fold_in(seeds[14], 71), 0)
    positions = draw_positions(jax.random.fold_in(seeds[14], 71), 0)
    attn_norm_gain = jnp.clip(1.0 + 0.18 * jax.random.normal(seeds[2], (MODEL_WIDTH,), jnp.float32), 0.099609375, 1.8984375).astype(jnp.bfloat16)
    w_query = centred(seeds[3], (MODEL_WIDTH, QUERY_HEADS * HEAD_SIZE), MODEL_WIDTH ** -0.5, 0.1875, ((0, 4),))
    key_projection = centred(seeds[4], (MODEL_WIDTH, KEY_VALUE_HEADS * HEAD_SIZE), MODEL_WIDTH ** -0.5, 0.1875, ((0, 4),))
    value_projection = centred(seeds[5], (MODEL_WIDTH, KEY_VALUE_HEADS * HEAD_SIZE), MODEL_WIDTH ** -0.5, 0.1875, ((0, 4),))
    query_norm_gain = draw_query_norm_gain(jax.random.fold_in(seeds[14], 71), 0)
    key_norm_gain = draw_key_norm_gain(jax.random.fold_in(seeds[14], 71), 0)
    output_projection = centred(seeds[8], (QUERY_HEADS * HEAD_SIZE, MODEL_WIDTH), (QUERY_HEADS * HEAD_SIZE // 32) ** -0.5, 0.75, ((0, 4),))
    ffn_norm_gain = jnp.clip(1.0 + 0.18 * jax.random.normal(seeds[9], (MODEL_WIDTH,), jnp.float32), 0.099609375, 1.8984375).astype(jnp.bfloat16)
    w_gate = centred(seeds[10], (MODEL_WIDTH, FF), MODEL_WIDTH ** -0.5, 0.1875, ((0, 4),))
    w_up = centred(seeds[11], (MODEL_WIDTH, FF), MODEL_WIDTH ** -0.5, 0.1875, ((0, 4),))
    w_down = centred(seeds[12], (FF, MODEL_WIDTH), FF ** -0.5, 0.109375, ((0, 4),))
    out_cotangent = centred(seeds[13], (SEQS, SEQUENCE_LENGTH, MODEL_WIDTH), 1.0, 6.0, ((0, 4), (1, 8)))
    return dict(block_input=block_input, positions=positions, attn_norm_gain=attn_norm_gain, w_query=w_query, key_projection=key_projection, value_projection=value_projection, query_norm_gain=query_norm_gain, key_norm_gain=key_norm_gain, output_projection=output_projection, ffn_norm_gain=ffn_norm_gain, w_gate=w_gate, w_up=w_up, w_down=w_down, out_cotangent=out_cotangent)


EPSILON = 1e-06
ROPE_BASE = 1000000.0
MASK_FLOOR = -1e+30

def inverse_rms(values):
    return lax.rsqrt(lax.optimization_barrier(jnp.mean(values * values, axis=-1, keepdims=True)) + EPSILON)

def norm_reverse(grad_out, values, inv_scale, gain_vector):
    gained = gain_vector * grad_out
    cubed = inv_scale * inv_scale * inv_scale
    return inv_scale * gained - values * cubed * lax.optimization_barrier(jnp.mean(gained * values, axis=-1, keepdims=True))

def rope_tables(places):
    half_dim = HEAD_SIZE // 2
    frequency = ROPE_BASE ** (-(jnp.arange(half_dim, dtype=jnp.float32) * 2.0 / HEAD_SIZE))
    angles = places.astype(jnp.float32)[:, None] * frequency[None, :]
    return (jnp.cos(angles)[:, None, :], jnp.sin(angles)[:, None, :])

def apply_rotary(values, cosine_lookup, sine_lookup):
    half_dim = HEAD_SIZE // 2
    first_half = values[..., :half_dim]
    second_half = values[..., half_dim:]
    return jnp.concatenate([first_half * cosine_lookup - second_half * sine_lookup, second_half * cosine_lookup + first_half * sine_lookup], axis=-1)

def reverse_rotary(grad_in, cosine_lookup, sine_lookup):
    half_dim = HEAD_SIZE // 2
    first_half = grad_in[..., :half_dim]
    second_half = grad_in[..., half_dim:]
    return jnp.concatenate([first_half * cosine_lookup + second_half * sine_lookup, second_half * cosine_lookup - first_half * sine_lookup], axis=-1)

def rounded_values(values):
    return lax.optimization_barrier(values.astype(jnp.bfloat16)).astype(jnp.float32)

def one_sequence(inputs_low, places, cotangent, weights):
    attn_gain, w_query, key_projection, value_projection, query_gain, key_gain, output_projection, ffn_gain, w_gate, w_up, w_down = weights
    query_groups = QUERY_HEADS // KEY_VALUE_HEADS
    key_window = min(512, SEQUENCE_LENGTH)
    query_span = SEQUENCE_LENGTH // N_CTX
    scale_factor = 1.0 / math.sqrt(HEAD_SIZE)
    inputs = inputs_low.astype(jnp.float32)
    gain_one = attn_gain.astype(jnp.float32)
    scale_one = inverse_rms(inputs)
    normalized_input = (inputs * scale_one * gain_one).astype(jnp.bfloat16)
    query_projected = jnp.dot(normalized_input, w_query, preferred_element_type=jnp.float32).reshape(SEQUENCE_LENGTH, QUERY_HEADS, HEAD_SIZE)
    key_projected = jnp.dot(normalized_input, key_projection, preferred_element_type=jnp.float32).reshape(SEQUENCE_LENGTH, KEY_VALUE_HEADS, HEAD_SIZE)
    value_complete = rounded_values(jnp.dot(normalized_input, value_projection, preferred_element_type=jnp.float32)).reshape(SEQUENCE_LENGTH, KEY_VALUE_HEADS, HEAD_SIZE)
    query_norm_scale = inverse_rms(query_projected)
    key_norm_scale = inverse_rms(key_projected)
    query_gain_wide32 = query_gain.astype(jnp.float32)
    key_gain_wide32 = key_gain.astype(jnp.float32)
    cosine_lookup, sine_lookup = rope_tables(places)
    query_complete = rounded_values(apply_rotary(query_projected * query_norm_scale * query_gain_wide32, cosine_lookup, sine_lookup)).reshape(SEQUENCE_LENGTH, KEY_VALUE_HEADS, query_groups, HEAD_SIZE)
    key_all = rounded_values(apply_rotary(key_projected * key_norm_scale * key_gain_wide32, cosine_lookup, sine_lookup))
    doc_starts = jnp.arange(SEQUENCE_LENGTH, dtype=jnp.int32) - places
    columns = jnp.arange(SEQUENCE_LENGTH, dtype=jnp.int32)

    def scores_of(row_offset, span):
        query_block = lax.dynamic_slice_in_dim(query_complete, row_offset, span, 0)
        row_ids = row_offset + jnp.arange(span, dtype=jnp.int32)
        starts = lax.dynamic_slice_in_dim(doc_starts, row_offset, span, 0)
        raw_scores = jnp.einsum('tkgd,skd->kgts', query_block, key_all) * scale_factor
        allowed = (columns[None, :] <= row_ids[:, None]) & (columns[None, :] >= starts[:, None])
        return (jnp.where(allowed, raw_scores, MASK_FLOOR), query_block)

    def attend(block_index):
        scores, query_block = scores_of(block_index * key_window, key_window)
        row_peak = lax.optimization_barrier(jnp.max(scores, axis=-1, keepdims=True))
        log_total = row_peak + jnp.log(lax.optimization_barrier(jnp.sum(jnp.exp(scores - row_peak), axis=-1, keepdims=True)))
        probability = rounded_values(jnp.exp(scores - log_total))
        weighted_sum = jnp.einsum('kgts,skd->tkgd', probability, value_complete)
        return (weighted_sum.reshape(key_window, QUERY_HEADS * HEAD_SIZE).astype(jnp.bfloat16), log_total[..., 0])
    blocks = jnp.arange(SEQUENCE_LENGTH // key_window, dtype=jnp.int32)
    attn_blocks, softmax_totals = lax.map(attend, blocks)
    softmax_totals_complete = jnp.transpose(softmax_totals, (1, 2, 0, 3)).reshape(KEY_VALUE_HEADS, query_groups, SEQUENCE_LENGTH)
    attention_output = lax.optimization_barrier(attn_blocks.reshape(SEQUENCE_LENGTH, QUERY_HEADS * HEAD_SIZE))
    middle = inputs + jnp.dot(attention_output, output_projection, preferred_element_type=jnp.float32)
    scale_two = inverse_rms(middle)
    gain_two = ffn_gain.astype(jnp.float32)
    normed_two = (middle * scale_two * gain_two).astype(jnp.bfloat16)
    gate_proj = jnp.dot(normed_two, w_gate, preferred_element_type=jnp.float32)
    upper = jnp.dot(normed_two, w_up, preferred_element_type=jnp.float32)
    gate_sigmoid = jax.nn.sigmoid(gate_proj)
    hidden = (gate_proj * gate_sigmoid * upper).astype(jnp.bfloat16)
    result = middle + jnp.dot(hidden, w_down, preferred_element_type=jnp.float32)
    block_out = result.astype(jnp.bfloat16)
    down_wgrad = jnp.dot(hidden.T, cotangent, preferred_element_type=jnp.float32)
    hidden_grad = jnp.dot(cotangent, w_down.T, preferred_element_type=jnp.float32)
    gate_grad = (hidden_grad * upper * gate_sigmoid * (1.0 + gate_proj * (1.0 - gate_sigmoid))).astype(jnp.bfloat16)
    up_grad = (hidden_grad * gate_proj * gate_sigmoid).astype(jnp.bfloat16)
    gate_wgrad = jnp.dot(normed_two.T, gate_grad, preferred_element_type=jnp.float32)
    up_wgrad = jnp.dot(normed_two.T, up_grad, preferred_element_type=jnp.float32)
    nt_grad = jnp.dot(gate_grad, w_gate.T, preferred_element_type=jnp.float32) + jnp.dot(up_grad, w_up.T, preferred_element_type=jnp.float32)
    ffn_gain_grad = lax.optimization_barrier(jnp.sum(nt_grad * middle * scale_two, axis=0))
    middle_grad = cotangent.astype(jnp.float32) + norm_reverse(nt_grad, middle, scale_two, gain_two)
    middle_narrow = middle_grad.astype(jnp.bfloat16)
    output_wgrad = jnp.dot(attention_output.T, middle_narrow, preferred_element_type=jnp.float32)
    attention_gradient = rounded_values(jnp.dot(middle_narrow, output_projection.T, preferred_element_type=jnp.float32)).reshape(SEQUENCE_LENGTH, KEY_VALUE_HEADS, query_groups, HEAD_SIZE)
    output_product = lax.optimization_barrier(jnp.sum(attention_gradient * attention_output.astype(jnp.float32).reshape(SEQUENCE_LENGTH, KEY_VALUE_HEADS, query_groups, HEAD_SIZE), axis=-1))
    output_product = jnp.transpose(output_product, (1, 2, 0))

    def back_step(state_now, block_index):
        key_grad, value_gradient = state_now
        row_offset = block_index * query_span
        scores, query_block = scores_of(row_offset, query_span)
        log_total = lax.dynamic_slice_in_dim(softmax_totals_complete, row_offset, query_span, 2)[..., None]
        probability = jnp.exp(scores - log_total)
        grad_block = lax.dynamic_slice_in_dim(attention_gradient, row_offset, query_span, 0)
        dot_block = lax.dynamic_slice_in_dim(output_product, row_offset, query_span, 2)
        value_gradient = value_gradient + rounded_values(jnp.einsum('kgts,tkgd->skd', rounded_values(probability), grad_block))
        prob_grad = jnp.einsum('tkgd,skd->kgts', grad_block, value_complete)
        score_grad = rounded_values(probability * (prob_grad - dot_block[..., None]))
        query_grad = jnp.einsum('kgts,skd->tkgd', score_grad, key_all) * scale_factor
        key_grad = key_grad + rounded_values(jnp.einsum('kgts,tkgd->skd', score_grad, query_block) * scale_factor)
        return ((key_grad, value_gradient), query_grad)
    empty_gradient = jnp.zeros((SEQUENCE_LENGTH, KEY_VALUE_HEADS, HEAD_SIZE), jnp.float32)
    query_blocks = jnp.arange(N_CTX, dtype=jnp.int32)
    (key_grad, value_gradient), query_grads = lax.scan(back_step, (empty_gradient, empty_gradient), query_blocks)
    query_grad = query_grads.reshape(SEQUENCE_LENGTH, QUERY_HEADS, HEAD_SIZE)
    query_pre = reverse_rotary(query_grad, cosine_lookup, sine_lookup)
    key_unnormed = reverse_rotary(key_grad, cosine_lookup, sine_lookup)
    query_gain_grad = lax.optimization_barrier(jnp.sum(query_pre * query_projected * query_norm_scale, axis=(0, 1)))
    key_gain_grad = lax.optimization_barrier(jnp.sum(key_unnormed * key_projected * key_norm_scale, axis=(0, 1)))
    query_low = norm_reverse(query_pre, query_projected, query_norm_scale, query_gain_wide32).reshape(SEQUENCE_LENGTH, QUERY_HEADS * HEAD_SIZE).astype(jnp.bfloat16)
    key_narrow = norm_reverse(key_unnormed, key_projected, key_norm_scale, key_gain_wide32).reshape(SEQUENCE_LENGTH, KEY_VALUE_HEADS * HEAD_SIZE).astype(jnp.bfloat16)
    value_narrow = value_gradient.reshape(SEQUENCE_LENGTH, KEY_VALUE_HEADS * HEAD_SIZE).astype(jnp.bfloat16)
    query_wgrad = jnp.dot(normalized_input.T, query_low, preferred_element_type=jnp.float32)
    key_wgrad = jnp.dot(normalized_input.T, key_narrow, preferred_element_type=jnp.float32)
    value_wgrad = jnp.dot(normalized_input.T, value_narrow, preferred_element_type=jnp.float32)
    normed_grad = jnp.dot(query_low, w_query.T, preferred_element_type=jnp.float32) + jnp.dot(key_narrow, key_projection.T, preferred_element_type=jnp.float32) + jnp.dot(value_narrow, value_projection.T, preferred_element_type=jnp.float32)
    attn_gain_grad = lax.optimization_barrier(jnp.sum(normed_grad * inputs * scale_one, axis=0))
    input_grad = middle_grad + norm_reverse(normed_grad, inputs, scale_one, gain_one)
    grad_terms = (attn_gain_grad, query_wgrad, key_wgrad, value_wgrad, query_gain_grad, key_gain_grad, output_wgrad, ffn_gain_grad, gate_wgrad, up_wgrad, down_wgrad)
    return (block_out, input_grad, grad_terms)

def reference(block_input, positions, attn_norm_gain, w_query, key_projection, value_projection, query_norm_gain, key_norm_gain, output_projection, ffn_norm_gain, w_gate, w_up, w_down, out_cotangent):
    weights = (attn_norm_gain, w_query, key_projection, value_projection, query_norm_gain, key_norm_gain, output_projection, ffn_norm_gain, w_gate, w_up, w_down)
    start_sums = tuple((jnp.zeros(matrix.shape, jnp.float32) for matrix in weights))

    def per_sequence(running, sequence):
        block_out, input_grad, grad_terms = one_sequence(block_input[sequence], positions[sequence], out_cotangent[sequence], weights)
        return (jax.tree.map(jnp.add, running, grad_terms), (block_out, input_grad))
    sums, (outputs, input_grads) = lax.scan(per_sequence, start_sums, jnp.arange(SEQS, dtype=jnp.int32))
    return (outputs, input_grads, sums[0], sums[1], sums[2], sums[3], sums[4], sums[5], sums[6], sums[7], sums[8], sums[9], sums[10])
```

```python
import math

import jax
import jax.numpy as jnp
from jax import lax
from jax.sharding import PartitionSpec as P

QUERY_HEADS = 16
KEY_VALUE_HEADS = 8
HEAD_SIZE = 128
FF = 3072


EPSILON = 1e-06
ROPE_BASE = 1000000.0
MASK_FLOOR = -1e30


def inverse_rms(values):
    return lax.rsqrt(jnp.mean(values * values, axis=-1, keepdims=True) + EPSILON)


def norm_reverse(grad_out, values, inv_scale, gain_vector):
    gained = gain_vector * grad_out
    cubed = inv_scale * inv_scale * inv_scale
    return inv_scale * gained - values * cubed * jnp.mean(gained * values, axis=-1, keepdims=True)


def rope_tables(places):
    half_dim = HEAD_SIZE // 2
    frequency = ROPE_BASE ** (-(jnp.arange(half_dim, dtype=jnp.float32) * 2.0 / HEAD_SIZE))
    angles = places.astype(jnp.float32)[:, None] * frequency[None, :]
    return (jnp.cos(angles)[:, None, :], jnp.sin(angles)[:, None, :])


def apply_rotary(values, cosine_lookup, sine_lookup):
    half_dim = HEAD_SIZE // 2
    first_half = values[..., :half_dim]
    second_half = values[..., half_dim:]
    return jnp.concatenate(
        [
            first_half * cosine_lookup - second_half * sine_lookup,
            second_half * cosine_lookup + first_half * sine_lookup,
        ],
        axis=-1,
    )


def reverse_rotary(grad_in, cosine_lookup, sine_lookup):
    half_dim = HEAD_SIZE // 2
    first_half = grad_in[..., :half_dim]
    second_half = grad_in[..., half_dim:]
    return jnp.concatenate(
        [
            first_half * cosine_lookup + second_half * sine_lookup,
            second_half * cosine_lookup - first_half * sine_lookup,
        ],
        axis=-1,
    )


def contract_rows(left, right):
    return lax.dot_general(
        left, right, (((0,), (0,)), ((), ())), preferred_element_type=jnp.float32
    )


def times_transpose(left, right):
    return lax.dot_general(
        left, right, (((1,), (1,)), ((), ())), preferred_element_type=jnp.float32
    )


def sum_blocks(row_shares):
    flat_terms = tuple((matrix.reshape(-1) for matrix in row_shares))
    pieces = lax.psum_scatter(flat_terms, "ctx", scatter_dimension=0, tiled=True)
    whole_rows = lax.all_gather(pieces, "ctx", axis=0, tiled=True)
    return tuple(
        (summed_part.reshape(matrix.shape) for summed_part, matrix in zip(whole_rows, row_shares))
    )


def local(
    block_input,
    positions,
    attn_norm_gain,
    w_query,
    key_projection,
    value_projection,
    query_norm_gain,
    key_norm_gain,
    output_projection,
    ffn_norm_gain,
    w_gate,
    w_up,
    w_down,
    out_cotangent,
):
    full_query, complete_key, full_value, full_output, full_gate, full_up, full_down = (
        lax.all_gather(w_query, "fsdp", axis=0, tiled=True),
        lax.all_gather(key_projection, "fsdp", axis=0, tiled=True),
        lax.all_gather(value_projection, "fsdp", axis=0, tiled=True),
        lax.all_gather(output_projection, "fsdp", axis=0, tiled=True),
        lax.all_gather(w_gate, "fsdp", axis=0, tiled=True),
        lax.all_gather(w_up, "fsdp", axis=0, tiled=True),
        lax.all_gather(w_down, "fsdp", axis=0, tiled=True),
    )
    token_count = block_input.shape[1]
    sequence_length = token_count * lax.axis_size("ctx")
    query_groups = QUERY_HEADS // KEY_VALUE_HEADS
    query_width = QUERY_HEADS * HEAD_SIZE
    group_width = KEY_VALUE_HEADS * HEAD_SIZE
    key_window = min(512, sequence_length)
    scale_factor = 1.0 / math.sqrt(HEAD_SIZE)
    inputs = block_input[0].astype(jnp.float32)
    places = positions[0]
    first_row = lax.axis_index("ctx") * token_count
    row_ids = first_row + jnp.arange(token_count, dtype=jnp.int32)
    doc_starts = row_ids - places
    gain_one = attn_norm_gain.astype(jnp.float32)
    scale_one = inverse_rms(inputs)
    normalized_input = (inputs * scale_one * gain_one).astype(jnp.bfloat16)
    query_projected = jnp.dot(
        normalized_input, full_query, preferred_element_type=jnp.float32
    ).reshape(token_count, QUERY_HEADS, HEAD_SIZE)
    key_projected = jnp.dot(
        normalized_input, complete_key, preferred_element_type=jnp.float32
    ).reshape(token_count, KEY_VALUE_HEADS, HEAD_SIZE)
    values = jnp.dot(normalized_input, full_value, preferred_element_type=jnp.float32).astype(
        jnp.bfloat16
    )
    query_norm_scale = inverse_rms(query_projected)
    key_norm_scale = inverse_rms(key_projected)
    query_gain_wide32 = query_norm_gain.astype(jnp.float32)
    key_gain_wide32 = key_norm_gain.astype(jnp.float32)
    cosine_lookup, sine_lookup = rope_tables(places)
    query_rot = (
        apply_rotary(
            query_projected * query_norm_scale * query_gain_wide32, cosine_lookup, sine_lookup
        )
        .astype(jnp.bfloat16)
        .reshape(token_count, KEY_VALUE_HEADS, query_groups, HEAD_SIZE)
    )
    key_rot = (
        apply_rotary(key_projected * key_norm_scale * key_gain_wide32, cosine_lookup, sine_lookup)
        .astype(jnp.bfloat16)
        .reshape(token_count, group_width)
    )
    all_keys, all_values = (
        lax.all_gather(key_rot, "ctx", axis=0, tiled=True),
        lax.all_gather(values, "ctx", axis=0, tiled=True),
    )
    lower_block = jnp.min(doc_starts) // key_window
    upper_block = (first_row + token_count - 1) // key_window + 1

    def fetch(block_index):
        token_shift = block_index * key_window
        key_block = lax.dynamic_slice_in_dim(all_keys, token_shift, key_window, 0).reshape(
            key_window, KEY_VALUE_HEADS, HEAD_SIZE
        )
        value_block = lax.dynamic_slice_in_dim(all_values, token_shift, key_window, 0).reshape(
            key_window, KEY_VALUE_HEADS, HEAD_SIZE
        )
        columns = token_shift + jnp.arange(key_window, dtype=jnp.int32)
        allowed = (columns[None, :] <= row_ids[:, None]) & (columns[None, :] >= doc_starts[:, None])
        scores = (
            jnp.einsum("tkgd,skd->kgts", query_rot, key_block, preferred_element_type=jnp.float32)
            * scale_factor
        )
        return (
            jnp.where(allowed, scores, MASK_FLOOR),
            key_block,
            value_block,
            token_shift,
            allowed,
        )

    def running_total(block_index, state_now):
        row_peak, running_sum = state_now
        scores, key_block, value_block, token_shift, allowed = fetch(block_index)
        new_peak = jnp.maximum(row_peak, jnp.max(scores, axis=-1))
        terms = jnp.where(allowed, jnp.exp(scores - new_peak[..., None]), 0.0)
        running_sum = running_sum * jnp.exp(row_peak - new_peak) + jnp.sum(terms, axis=-1)
        return (new_peak, running_sum)

    initial_peak = jnp.full((KEY_VALUE_HEADS, query_groups, token_count), MASK_FLOOR, jnp.float32)
    row_peak, running_sum = lax.fori_loop(
        lower_block, upper_block, running_total, (initial_peak, jnp.zeros_like(initial_peak))
    )
    log_total = row_peak + jnp.log(running_sum)

    def weighted_values(block_index, weighted_sum):
        scores, key_block, value_block, token_shift, allowed = fetch(block_index)
        probability = jnp.exp(scores - log_total[..., None]).astype(jnp.bfloat16)
        return weighted_sum + jnp.einsum(
            "kgts,skd->tkgd", probability, value_block, preferred_element_type=jnp.float32
        )

    weighted_sum = lax.fori_loop(
        lower_block,
        upper_block,
        weighted_values,
        jnp.zeros((token_count, KEY_VALUE_HEADS, query_groups, HEAD_SIZE), jnp.float32),
    )
    attention_output = weighted_sum.reshape(token_count, query_width).astype(jnp.bfloat16)
    middle = inputs + jnp.dot(attention_output, full_output, preferred_element_type=jnp.float32)
    scale_two = inverse_rms(middle)
    gain_two = ffn_norm_gain.astype(jnp.float32)
    normed_two = (middle * scale_two * gain_two).astype(jnp.bfloat16)
    gate_proj = jnp.dot(normed_two, full_gate, preferred_element_type=jnp.float32)
    upper = jnp.dot(normed_two, full_up, preferred_element_type=jnp.float32)
    gate_sigmoid = jax.nn.sigmoid(gate_proj)
    hidden = (gate_proj * gate_sigmoid * upper).astype(jnp.bfloat16)
    result = middle + jnp.dot(hidden, full_down, preferred_element_type=jnp.float32)
    block_output = result.astype(jnp.bfloat16)[None]
    back_query, back_key, back_value = (full_query, complete_key, full_value)
    back_output, back_gate, back_up, back_down = (full_output, full_gate, full_up, full_down)
    cotangent = out_cotangent[0]
    hidden_grad = times_transpose(cotangent, back_down)
    gate_grad = (
        hidden_grad * upper * gate_sigmoid * (1.0 + gate_proj * (1.0 - gate_sigmoid))
    ).astype(jnp.bfloat16)
    up_grad = (hidden_grad * gate_proj * gate_sigmoid).astype(jnp.bfloat16)
    nt_grad = times_transpose(gate_grad, back_gate) + times_transpose(up_grad, back_up)
    ffn_gain_term = jnp.sum(nt_grad * middle * scale_two, axis=0)
    middle_grad = cotangent.astype(jnp.float32) + norm_reverse(nt_grad, middle, scale_two, gain_two)
    middle_narrow = middle_grad.astype(jnp.bfloat16)
    down_rows = lax.psum_scatter(
        contract_rows(hidden, cotangent), "fsdp", scatter_dimension=0, tiled=True
    )
    output_rows = lax.psum_scatter(
        contract_rows(attention_output, middle_narrow), "fsdp", scatter_dimension=0, tiled=True
    )
    attention_gradient = (
        times_transpose(middle_narrow, back_output)
        .astype(jnp.bfloat16)
        .reshape(token_count, KEY_VALUE_HEADS, query_groups, HEAD_SIZE)
    )
    output_product = jnp.sum(
        attention_gradient.astype(jnp.float32)
        * attention_output.astype(jnp.float32).reshape(
            token_count, KEY_VALUE_HEADS, query_groups, HEAD_SIZE
        ),
        axis=-1,
    )
    output_product = jnp.transpose(output_product, (1, 2, 0))

    def back_block(block_index, state_now):
        query_grad, key_contributions, value_contributions = state_now
        scores, key_block, value_block, token_shift, allowed = fetch(block_index)
        probability = jnp.exp(scores - log_total[..., None])
        value_portion = jnp.einsum(
            "kgts,tkgd->skd",
            probability.astype(jnp.bfloat16),
            attention_gradient,
            preferred_element_type=jnp.float32,
        )
        prob_grad = jnp.einsum(
            "tkgd,skd->kgts", attention_gradient, value_block, preferred_element_type=jnp.float32
        )
        score_grad = (probability * (prob_grad - output_product[..., None])).astype(jnp.bfloat16)
        query_grad = (
            query_grad
            + jnp.einsum(
                "kgts,skd->tkgd", score_grad, key_block, preferred_element_type=jnp.float32
            )
            * scale_factor
        )
        key_portion = (
            jnp.einsum("kgts,tkgd->skd", score_grad, query_rot, preferred_element_type=jnp.float32)
            * scale_factor
        )
        key_previous = lax.dynamic_slice_in_dim(key_contributions, token_shift, key_window, 0)
        key_contributions = lax.dynamic_update_slice_in_dim(
            key_contributions,
            key_previous + key_portion.reshape(key_window, group_width),
            token_shift,
            0,
        )
        value_previous = lax.dynamic_slice_in_dim(value_contributions, token_shift, key_window, 0)
        value_contributions = lax.dynamic_update_slice_in_dim(
            value_contributions,
            value_previous + value_portion.reshape(key_window, group_width),
            token_shift,
            0,
        )
        return (query_grad, key_contributions, value_contributions)

    empty_keys = jnp.zeros((sequence_length, group_width), jnp.float32)
    query_grad, key_contributions, value_contributions = lax.fori_loop(
        lower_block,
        upper_block,
        back_block,
        (
            jnp.zeros((token_count, KEY_VALUE_HEADS, query_groups, HEAD_SIZE), jnp.float32),
            empty_keys,
            empty_keys,
        ),
    )
    key_total_sum, value_sum = (
        lax.psum_scatter(
            key_contributions.astype(jnp.bfloat16), "ctx", scatter_dimension=0, tiled=True
        ).astype(jnp.float32),
        lax.psum_scatter(
            value_contributions.astype(jnp.bfloat16), "ctx", scatter_dimension=0, tiled=True
        ).astype(jnp.float32),
    )
    query_pre = reverse_rotary(
        query_grad.reshape(token_count, QUERY_HEADS, HEAD_SIZE), cosine_lookup, sine_lookup
    )
    key_unnormed = reverse_rotary(
        key_total_sum.reshape(token_count, KEY_VALUE_HEADS, HEAD_SIZE), cosine_lookup, sine_lookup
    )
    query_gain_term = jnp.sum(query_pre * query_projected * query_norm_scale, axis=(0, 1))
    key_gain_term = jnp.sum(key_unnormed * key_projected * key_norm_scale, axis=(0, 1))
    query_low = (
        norm_reverse(query_pre, query_projected, query_norm_scale, query_gain_wide32)
        .reshape(token_count, query_width)
        .astype(jnp.bfloat16)
    )
    key_narrow = (
        norm_reverse(key_unnormed, key_projected, key_norm_scale, key_gain_wide32)
        .reshape(token_count, group_width)
        .astype(jnp.bfloat16)
    )
    value_narrow = value_sum.astype(jnp.bfloat16)
    normed_grad = (
        times_transpose(query_low, back_query)
        + times_transpose(key_narrow, back_key)
        + times_transpose(value_narrow, back_value)
    )
    attn_gain_term = jnp.sum(normed_grad * inputs * scale_one, axis=0)
    input_grad = middle_grad + norm_reverse(normed_grad, inputs, scale_one, gain_one)
    attn_side = jnp.concatenate([query_low, key_narrow, value_narrow], axis=1)
    ffn_side = jnp.concatenate([gate_grad, up_grad], axis=1)
    first_part = contract_rows(normalized_input, attn_side)
    second_part = contract_rows(normed_two, ffn_side)
    input_rows = lax.psum_scatter(
        jnp.concatenate([first_part, second_part], axis=1), "fsdp", scatter_dimension=0, tiled=True
    )
    input_sum, output_sum, down_sum = sum_blocks((input_rows, output_rows, down_rows))
    query_sum = input_sum[:, :query_width]
    key_wsum = input_sum[:, query_width : query_width + group_width]
    value_wsum = input_sum[:, query_width + group_width : query_width + 2 * group_width]
    gate_sum = input_sum[:, query_width + 2 * group_width : query_width + 2 * group_width + FF]
    up_sum = input_sum[:, query_width + 2 * group_width + FF :]
    gain_sums = lax.psum(
        (attn_gain_term, query_gain_term, key_gain_term, ffn_gain_term), ("fsdp", "ctx")
    )
    return (
        block_output,
        input_grad[None],
        gain_sums[0],
        query_sum,
        key_wsum,
        value_wsum,
        gain_sums[1],
        gain_sums[2],
        output_sum,
        gain_sums[3],
        gate_sum,
        up_sum,
        down_sum,
    )


def split_low(values):
    high = lax.reduce_precision(values, 8, 7)
    return high.astype(jnp.bfloat16), (values - high).astype(jnp.bfloat16)


def fold_columns(pieces):
    count, rows, width = pieces.shape
    half = rows // 2
    parts = [pieces[:, :, at : at + 1024] for at in range(0, width - 1023, 1024)]
    if width % 1024:
        rest = pieces[:, :, width - 512 :]
        parts.append(jnp.concatenate([rest[:, :half], rest[:, half:]], axis=2))
    return jnp.concatenate(parts, axis=1) if len(parts) > 1 else parts[0]


def unfold_columns(folded, rows, width):
    parts = [folded[:, at * rows : (at + 1) * rows] for at in range(width // 1024)]
    if width % 1024:
        rest = folded[:, (width // 1024) * rows :]
        parts.append(jnp.concatenate([rest[:, :, :512], rest[:, :, 512:]], axis=1))
    return jnp.concatenate(parts, axis=2) if len(parts) > 1 else parts[0]


def local_by_heads(
    block_input,
    positions,
    attn_norm_gain,
    w_query,
    key_projection,
    value_projection,
    query_norm_gain,
    key_norm_gain,
    output_projection,
    ffn_norm_gain,
    w_gate,
    w_up,
    w_down,
    out_cotangent,
):
    shards = lax.axis_size("fsdp")
    blocks = lax.axis_size("ctx")
    span = block_input.shape[1]
    width = block_input.shape[2]
    tokens = shards * span
    length = blocks * span
    groups = QUERY_HEADS // KEY_VALUE_HEADS
    kv_heads = KEY_VALUE_HEADS // shards
    q_heads = kv_heads * groups
    q_cols = q_heads * HEAD_SIZE
    kv_cols = kv_heads * HEAD_SIZE
    ff_cols = FF // shards
    scale_factor = 1.0 / math.sqrt(HEAD_SIZE)
    low = jnp.bfloat16
    f32 = jnp.float32

    place = positions[0][:, None]
    codes = jnp.concatenate([place // 32, place % 32], axis=1).astype(low)
    packed = jnp.concatenate(
        [block_input[0], out_cotangent[0], jnp.pad(codes, ((0, 0), (0, 126)))], axis=1
    )
    packed = lax.all_gather(packed, "fsdp", axis=0, tiled=True)
    inputs = packed[:, :width].astype(f32)
    cotangent = packed[:, width : 2 * width]
    codes = packed[:, 2 * width : 2 * width + 2].astype(jnp.int32)
    places = codes[:, 0] * 32 + codes[:, 1]

    def by_columns(*matrices):
        rows = matrices[0].shape[0]
        cut = jnp.concatenate([m.reshape(rows, shards, -1) for m in matrices], axis=2)
        cut = jnp.transpose(cut, (1, 0, 2))
        cut = lax.all_to_all(cut, "fsdp", split_axis=0, concat_axis=0, tiled=True)
        return cut.reshape(shards * rows, -1)

    attn_weights = by_columns(w_query, key_projection, value_projection)
    ffn_weights = by_columns(w_gate, w_up)

    gain_one = attn_norm_gain.astype(f32)
    scale_one = inverse_rms(inputs)
    normed = (inputs * scale_one * gain_one).astype(low)
    projected = jnp.dot(normed, attn_weights, preferred_element_type=f32)
    query = projected[:, :q_cols].reshape(tokens, q_heads, HEAD_SIZE)
    key = projected[:, q_cols : q_cols + kv_cols].reshape(tokens, kv_heads, HEAD_SIZE)
    value = projected[:, q_cols + kv_cols :].astype(low)
    query_scale = inverse_rms(query)
    key_scale = inverse_rms(key)
    query_gain = query_norm_gain.astype(f32)
    key_gain = key_norm_gain.astype(f32)
    cosine, sine = rope_tables(places)
    query_rot = apply_rotary(query * query_scale * query_gain, cosine, sine).astype(low)
    key_rot = apply_rotary(key * key_scale * key_gain, cosine, sine).astype(low)
    both = jnp.concatenate([key_rot.reshape(tokens, kv_cols), value], axis=1)
    both = lax.all_gather(both, "ctx", axis=0)
    both = both.reshape(blocks, shards, span, 2, kv_heads, HEAD_SIZE)
    both = jnp.transpose(both, (3, 1, 4, 0, 2, 5)).reshape(2, shards, kv_heads, length, HEAD_SIZE)
    all_keys, all_values = both[0], both[1]

    def per_kv(array):
        array = array.reshape(shards, span, kv_heads, groups, HEAD_SIZE)
        return jnp.transpose(array, (0, 2, 3, 1, 4)).reshape(
            shards, kv_heads, groups * span, HEAD_SIZE
        )

    def per_token(array):
        array = array.reshape(shards, kv_heads, groups, span, HEAD_SIZE)
        return jnp.transpose(array, (0, 3, 1, 2, 4)).reshape(tokens, q_cols)

    query_kv = per_kv(query_rot)
    row_ids = lax.axis_index("ctx") * span + jnp.arange(span, dtype=jnp.int32)
    starts = row_ids[None, :] - places.reshape(shards, span)
    columns = jnp.arange(length, dtype=jnp.int32)
    allowed = (columns <= row_ids[None, :, None]) & (columns >= starts[:, :, None])
    allowed = jnp.broadcast_to(
        allowed[:, None, None], (shards, 1, groups, span, length)
    ).reshape(shards, 1, groups * span, length)
    scores = jnp.einsum("skqd,skjd->skqj", query_kv, all_keys, preferred_element_type=f32)
    scores = jnp.where(allowed, scores * scale_factor, MASK_FLOOR)
    peak = jnp.max(scores, axis=-1, keepdims=True)
    log_total = peak + jnp.log(jnp.sum(jnp.exp(scores - peak), axis=-1, keepdims=True))
    probability = jnp.exp(scores - log_total)
    probability_low = probability.astype(low)
    attended = jnp.einsum(
        "skqj,skjd->skqd", probability_low, all_values, preferred_element_type=f32
    ).astype(low)
    attention_output = per_token(attended)
    partial = jnp.dot(attention_output, output_projection, preferred_element_type=f32)
    middle = block_input[0].astype(f32) + lax.psum_scatter(
        partial, "fsdp", scatter_dimension=0, tiled=True
    )
    scale_two = inverse_rms(middle)
    gain_two = ffn_norm_gain.astype(f32)
    normed_two = lax.all_gather(
        (middle * scale_two * gain_two).astype(low), "fsdp", axis=0, tiled=True
    )
    wide = jnp.dot(normed_two, ffn_weights, preferred_element_type=f32)
    gate, upper = wide[:, :ff_cols], wide[:, ff_cols:]
    sigmoid = jax.nn.sigmoid(gate)
    hidden = (gate * sigmoid * upper).astype(low)
    down_partial = jnp.dot(hidden, w_down, preferred_element_type=f32)
    hidden_grad = times_transpose(cotangent, w_down)
    gate_grad = (hidden_grad * upper * sigmoid * (1.0 + gate * (1.0 - sigmoid))).astype(low)
    up_grad = (hidden_grad * gate * sigmoid).astype(low)
    ffn_side = jnp.concatenate([gate_grad, up_grad], axis=1)
    nt_partial = times_transpose(ffn_side, ffn_weights)
    pair = jnp.concatenate([down_partial, nt_partial], axis=1).astype(low)
    pair = lax.psum_scatter(pair, "fsdp", scatter_dimension=0, tiled=True).astype(f32)
    block_output = (middle + pair[:, :width]).astype(low)[None]
    nt_grad = pair[:, width:]
    ffn_gain_term = jnp.sum(nt_grad * middle * scale_two, axis=0)
    middle_grad = out_cotangent[0].astype(f32) + norm_reverse(
        nt_grad, middle, scale_two, gain_two
    )
    middle_low = lax.all_gather(middle_grad.astype(low), "fsdp", axis=0, tiled=True)

    piece = width // shards // blocks

    def piece_order(array):
        array = array.reshape(tokens, shards, blocks, piece)
        return jnp.transpose(array, (0, 2, 1, 3)).reshape(tokens, width)

    def ctx_sum(*pieces):
        stacked = jnp.concatenate(pieces, axis=1)
        rows = stacked.shape[1]
        stacked = stacked.reshape(blocks * rows, width)
        return lax.psum_scatter(stacked, "ctx", scatter_dimension=0, tiled=True)

    ffn_grads = contract_rows(piece_order(normed_two), ffn_side).astype(low)
    down_grads = contract_rows(hidden, cotangent).astype(low)
    ffn_piece = ctx_sum(
        fold_columns(ffn_grads.reshape(blocks, shards * piece, 2 * ff_cols)),
        down_grads.reshape(blocks, ff_cols // blocks, width),
    )

    attn_grad = per_kv(times_transpose(middle_low, output_projection).astype(low))
    delta = jnp.sum(attn_grad.astype(f32) * attended.astype(f32), axis=-1, keepdims=True)
    value_part = jnp.einsum(
        "skqj,skqd->skjd", probability_low, attn_grad, preferred_element_type=f32
    )
    prob_grad = jnp.einsum("skqd,skjd->skqj", attn_grad, all_values, preferred_element_type=f32)
    score_grad = (probability * (prob_grad - delta)).astype(low)
    query_back = (
        jnp.einsum("skqj,skjd->skqd", score_grad, all_keys, preferred_element_type=f32)
        * scale_factor
    )
    key_part = (
        jnp.einsum("skqj,skqd->skjd", score_grad, query_kv, preferred_element_type=f32)
        * scale_factor
    )
    parts = jnp.stack([key_part, value_part]).astype(low)
    parts = parts.reshape(2, shards, kv_heads, blocks, span, HEAD_SIZE)
    parts = jnp.transpose(parts, (3, 1, 4, 0, 2, 5)).reshape(blocks * tokens, 2 * kv_cols)
    sums = lax.psum_scatter(parts, "ctx", scatter_dimension=0, tiled=True).astype(f32)
    query_pre = reverse_rotary(
        per_token(query_back).reshape(tokens, q_heads, HEAD_SIZE), cosine, sine
    )
    key_pre = reverse_rotary(
        sums[:, :kv_cols].reshape(tokens, kv_heads, HEAD_SIZE), cosine, sine
    )
    query_gain_term = jnp.sum(query_pre * query * query_scale, axis=(0, 1))
    key_gain_term = jnp.sum(key_pre * key * key_scale, axis=(0, 1))
    query_low = norm_reverse(query_pre, query, query_scale, query_gain).reshape(tokens, q_cols)
    key_low = norm_reverse(key_pre, key, key_scale, key_gain).reshape(tokens, kv_cols)
    attn_side = jnp.concatenate(
        [query_low.astype(low), key_low.astype(low), sums[:, kv_cols:].astype(low)], axis=1
    )
    normed_partial = times_transpose(attn_side, attn_weights)
    attn_gain_term = jnp.sum(normed_partial * inputs * scale_one, axis=0)
    normed_grad = lax.psum_scatter(
        normed_partial.astype(low), "fsdp", scatter_dimension=0, tiled=True
    ).astype(f32)
    own = block_input[0].astype(f32)
    input_grad = middle_grad + norm_reverse(normed_grad, own, inverse_rms(own), gain_one)

    side_cols = q_cols + 2 * kv_cols
    attn_grads = contract_rows(piece_order(normed), attn_side).astype(low)
    output_grads = contract_rows(attention_output, middle_low).astype(low)
    attn_piece = ctx_sum(
        fold_columns(attn_grads.reshape(blocks, shards * piece, side_cols)),
        output_grads.reshape(blocks, q_cols // blocks, width),
    )

    def rows_of(array, rows, cols):
        return fold_columns(unfold_columns(array[None], rows, cols).reshape(shards, piece, cols))

    ffn_rows = shards * piece * 2 * ff_cols // width
    attn_rows = shards * piece * side_cols // width
    gains = jnp.concatenate(
        [
            attn_gain_term,
            ffn_gain_term,
            query_gain_term,
            key_gain_term,
            jnp.zeros((2 * width - 2 * HEAD_SIZE,), f32),
        ]
    ).reshape(4, width)

    def gain_rows(values):
        return jnp.concatenate(split_low(values), axis=-2)

    def gain_values(rows):
        wide_rows = rows.astype(f32)
        return wide_rows[..., :4, :] + wide_rows[..., 4:, :]

    outgoing = jnp.concatenate(
        [
            rows_of(attn_piece[:attn_rows], shards * piece, side_cols),
            rows_of(ffn_piece[:ffn_rows], shards * piece, 2 * ff_cols),
            jnp.broadcast_to(gain_rows(gains)[None], (shards, 8, width)),
        ],
        axis=1,
    )
    arrived = lax.all_to_all(outgoing, "fsdp", split_axis=0, concat_axis=0, tiled=True)
    mixed = arrived.shape[1] - 8
    shard_gains = jnp.sum(gain_values(arrived[:, mixed:]), axis=0)
    final = jnp.concatenate(
        [
            arrived[:, :mixed].reshape(shards * mixed, width),
            attn_piece[attn_rows:],
            ffn_piece[ffn_rows:],
            gain_rows(shard_gains),
        ],
        axis=0,
    )
    final = lax.all_gather(final, "ctx", axis=0)
    top = shards * mixed
    matrices = final[:, :top].reshape(blocks * shards, mixed, width)
    attn_in = piece * side_cols // width
    attn_all = unfold_columns(matrices[:, :attn_in], piece, side_cols)
    ffn_all = unfold_columns(matrices[:, attn_in:], piece, 2 * ff_cols)

    def whole(array, first, last):
        array = array[:, :, first:last].reshape(blocks, shards, piece, last - first)
        array = jnp.transpose(array, (0, 2, 1, 3)).astype(f32)
        return array.reshape(blocks * piece, shards * (last - first))

    out_rows = q_cols // blocks
    down_rows = ff_cols // blocks
    output_sum = final[:, top : top + out_rows].reshape(q_cols, width).astype(f32)
    down_sum = (
        final[:, top + out_rows : top + out_rows + down_rows].reshape(ff_cols, width).astype(f32)
    )
    gain_sums = jnp.sum(gain_values(final[:, top + out_rows + down_rows :]), axis=0)
    return (
        block_output,
        input_grad[None],
        gain_sums[0],
        whole(attn_all, 0, q_cols),
        whole(attn_all, q_cols, q_cols + kv_cols),
        whole(attn_all, q_cols + kv_cols, side_cols),
        gain_sums[2, :HEAD_SIZE],
        gain_sums[2, HEAD_SIZE : 2 * HEAD_SIZE],
        output_sum,
        gain_sums[1],
        whole(ffn_all, 0, ff_cols),
        whole(ffn_all, ff_cols, 2 * ff_cols),
        down_sum,
    )


def solution(mesh):
    shards, blocks = mesh.shape["fsdp"], mesh.shape["ctx"]
    split_heads = shards == 4 and blocks == 8
    return jax.shard_map(
        local_by_heads if split_heads else local,
        mesh=mesh,
        in_specs=(
            P("fsdp", "ctx", None),
            P("fsdp", "ctx"),
            P(),
            P("fsdp", None),
            P("fsdp", None),
            P("fsdp", None),
            P(),
            P(),
            P("fsdp", None),
            P(),
            P("fsdp", None),
            P("fsdp", None),
            P("fsdp", None),
            P("fsdp", "ctx", None),
        ),
        out_specs=(
            P("fsdp", "ctx", None),
            P("fsdp", "ctx", None),
            P(),
            P("fsdp", None),
            P("fsdp", None),
            P("fsdp", None),
            P(),
            P(),
            P("fsdp", None),
            P(),
            P("fsdp", None),
            P("fsdp", None),
            P("fsdp", None),
        ),
        check_vma=False,
    )
```
